32 devices in a mesh: groups: 2 (over x), dp: 16 (over z, y, core).
Axes of the slice: x: 2, y: 2, z: 4, core: 2. Of those that a mesh axis runs over, the one named last changes fastest.
Arguments:
- tokens: bfloat16 [2048, 3072], P(('groups', 'dp')), parts along dimension 0, may hold values from -6 to 6
- router: bfloat16 [3072, 4], replicated, may hold values from -0.109375 to 0.109375
- routes: int32 [2048, 2], P(('groups', 'dp')), parts along dimension 0, may hold values from 0 to 3, all different within a row; in each aligned block of 64 rows (0 to 63, 64 to 127, ...) at most 36 rows name the same one
- w_gate: bfloat16 [3072, 32768], P(None, 'dp'), may hold values from -0.109375 to 0.109375
- w_up: bfloat16 [3072, 32768], P(None, 'dp'), may hold values from -0.109375 to 0.109375
- w_down: bfloat16 [32768, 3072], P('dp'), may hold values from -0.0625 to 0.0625
Outputs:
- mixed: bfloat16 [2048, 3072], P(('groups', 'dp')), parts along dimension 0
The draws below stay inside these ranges and needn't reach their ends.
There are 2 independent parts, one for each index of `groups`. The reference program is written for one: setup_inputs(seed, part) draws one part's arguments, and reference() takes and returns one part's arrays. A program takes and returns all parts, laid end to end along the dimension named above; an argument that names none is the same for every part. Nothing has to cross between parts.
Inputs may be any that keep to these rules, and one draw needn't show every extreme that they name: `routes`: each token names 2 different experts; within the rows of one device no expert is named by more than 36 rows, a bound that some block reaches.
All inputs are finite; a program needn't handle non-finite values.
Results may differ from the reference program's by a relative error of at most 0.0058.
Values may be sent and summed in bfloat16 or wider, within the bound.
A program may use at most 128 MiB of HBM per device.

```python
import math
import jax
import jax.numpy as jnp
import numpy as np

D = 3072
FF = 8192
E = 4
TOP = 2
TOK_DEV = 64
CAP = 36
TOKENS = 1024
MEMBERS = 4
FF_DEV = 2048
N_DP = 16


def block_scale(rng, dims, split, smallest, top_value):
    factor_of = 1.0
    for axis_at, parts in split:
        draws = jax.random.uniform(jax.random.fold_in(jax.random.fold_in(rng, 6), axis_at), (parts,), jnp.float32, smallest / len(split), top_value / len(split))
        factor_of = factor_of * jnp.repeat(jnp.exp(draws), dims[axis_at] // parts).reshape((-1,) + (1,) * (len(dims) - 1 - axis_at))
    return factor_of


def routed_block(key, own, number, rows, count, top, bound, slope):
    ranking = jax.random.permutation(key, count)
    heavy_load, usual = load_shares(count, rows * top, bound, slope, True), load_shares(count, rows * top, bound, slope, False)
    places = jnp.arange(count)

    def named(sizes, turn):
        used = int((sizes > 0).sum())
        fixed = max(1, used // 4)
        moved = fixed + (places - fixed + turn * (used - fixed)) % max(1, count - fixed)
        return jnp.zeros((count,), jnp.int32).at[ranking[jnp.where(places < fixed, places, moved)]].set(jnp.asarray(sizes, jnp.int32))

    sizes = jnp.where(number % 4 == 0, named(heavy_load, number // 4), named(usual, number - number // 4 - 1))
    mixed = jax.random.permutation(jax.random.fold_in(own, 3), count)
    giver, sink = mixed[0:count // 2 * 2:2], mixed[1:count // 2 * 2:2]
    room = jnp.minimum(sizes[giver] - 1, bound - sizes[sink]) // 2
    room = jnp.where((giver == ranking[0]) | (sink == ranking[0]) | (sizes[sink] == 0), 0, jnp.maximum(room, 0))
    moved = jax.random.randint(jax.random.fold_in(own, 4), (count // 2,), 0, 1 << 20) % (room + 1)
    sizes = sizes.at[giver].add(-moved).at[sink].add(moved)
    items = jnp.searchsorted(jnp.cumsum(sizes), jnp.arange(rows * top), side="right").astype(jnp.int32)
    table = items.reshape(top, rows).T
    table = table[jax.random.permutation(jax.random.fold_in(own, 1), rows)]
    turn = jax.random.randint(jax.random.fold_in(own, 2), (rows, 1), 0, top)
    return jnp.take_along_axis(table, (jnp.arange(top)[None, :] + turn) % top, axis=1)


def load_shares(count, total, most, lean, full):
    weights = [(1 << 20) // math.isqrt(standing ** lean) + 1 for standing in range(1, count + 1)]
    largest = most if full else min(most, max(-(-total // count), total * weights[0] // sum(weights)))
    least = 1 if total - largest >= count - 1 else 0
    counts, spare = [largest] + [least] * (count - 1), total - largest - least * (count - 1)
    while spare > 0:
        free = [i for i in range(1, count) if counts[i] < largest] or [i for i in range(1, count) if counts[i] < most]
        mass, budget = sum([weights[i] for i in free]), spare
        for i in free:
            more = min(most - counts[i], max(1, budget * weights[i] // mass), spare)
            counts[i] = counts[i] + more
            spare = spare - more
    return np.array(counts)


def normal_values(rng, shape, width, most, shards=(), kind=jnp.bfloat16):
    values = jax.random.normal(rng, shape, jnp.float32) * width
    if len(shards) > 0:
        values = block_scale(rng, shape, shards, -0.22, 0.18) * values
    return jnp.clip(values, min=-most, max=most).astype(kind)


def setup_inputs(seed: int = 0, part: int = 0) -> dict:
    key_list = jax.random.split(jax.random.key(seed), 7)
    part_keys = jax.random.split(jax.random.fold_in(key_list[6], part), 7)
    tokens = normal_values(part_keys[0], (TOKENS, D), 1.0, 6.0, ((0, 16),))
    router = normal_values(key_list[1], (D, E), D ** -0.5, 0.109375)
    routes_keys = jax.random.split(jax.random.fold_in(part_keys[2], 1), TOKENS // TOK_DEV)
    routes_turns = jax.random.permutation(jax.random.fold_in(part_keys[2], 3), TOKENS // TOK_DEV)
    routes = jax.vmap(lambda own, number: routed_block(jax.random.fold_in(part_keys[2], 2), own, number, TOK_DEV, E, TOP, CAP, 2))(routes_keys, routes_turns).reshape((TOKENS, TOP))
    w_gate = normal_values(key_list[3], (D, E * FF), D ** -0.5, 0.109375, ((1, 16),))
    w_up = normal_values(key_list[4], (D, E * FF), D ** -0.5, 0.109375, ((1, 16),))
    w_down = normal_values(key_list[5], (E * FF, D), FF ** -0.5, 0.0625, ((0, 16),))
    return {"tokens": tokens, "router": router, "routes": routes, "w_gate": w_gate, "w_up": w_up, "w_down": w_down}


def run_expert(picked_rows, gate_cols, up_cols, down_rows):
    gate_vals = jnp.dot(picked_rows, gate_cols, preferred_element_type=jnp.float32)
    up_vals = jnp.dot(picked_rows, up_cols, preferred_element_type=jnp.float32)
    hidden = (jax.nn.silu(gate_vals) * up_vals).astype(jnp.bfloat16)
    total = jnp.zeros((picked_rows.shape[0], down_rows.shape[1]), jnp.float32)
    for member in range(MEMBERS):
        lower = member * FF_DEV
        piece = jnp.dot(hidden[:, lower:lower + FF_DEV], down_rows[lower:lower + FF_DEV, :],
                        preferred_element_type=jnp.float32).astype(jnp.bfloat16)
        total = total + piece.astype(jnp.float32)
    return total


def reference(tokens, router, routes, w_gate, w_up, w_down):
    logits = jnp.dot(tokens, router, preferred_element_type=jnp.float32)
    picked = jnp.take_along_axis(logits, routes, axis=1)
    first_share = jax.nn.sigmoid(picked[:, 0] - picked[:, 1])
    shares = jnp.stack([first_share, 1.0 - first_share], axis=1)
    flat_ids = routes.reshape(-1).astype(jnp.int32)
    positions = jnp.arange(TOKENS * TOP, dtype=jnp.int32)
    owner_rows = positions // TOP
    flat_shares = shares.reshape(-1)
    limit_rows = N_DP * CAP
    combined = jnp.zeros((TOKENS, D), jnp.float32)
    for expert in range(E):
        sort_key = jnp.where(flat_ids == expert, positions, TOKENS * TOP + positions)
        ordering = jnp.argsort(sort_key)[:limit_rows].astype(jnp.int32)
        matches = (flat_ids[ordering] == expert).astype(jnp.float32)
        chosen_rows = owner_rows[ordering]
        picked_rows = tokens[chosen_rows]
        expert_out = run_expert(picked_rows, w_gate[:, expert * FF:(expert + 1) * FF],
                                w_up[:, expert * FF:(expert + 1) * FF],
                                w_down[expert * FF:(expert + 1) * FF, :])
        scaled = expert_out * (flat_shares[ordering] * matches)[:, None]
        combined = combined.at[chosen_rows].add(scaled)
    return combined.astype(jnp.bfloat16)
```

```python
import functools

import jax
import jax.numpy as jnp
from jax import lax
from jax.experimental import pallas as pl
from jax.experimental.pallas import tpu as pltpu
from jax.sharding import PartitionSpec as P

CAP = 36
MAIN = 32
TAIL = CAP - MAIN
PIECES = 16 // TAIL
MESH = pl.DeviceIdType.MESH
TILE = 256


def moe_kernel(experts, chips, pa, pb, wg_hbm, wu_hbm, wd_hbm, ra, rb,
               wg, wu, wd, xf, xb, hid, cra, crb, yra, yrb, zsa, zsb,
               load_sem, own_sem, z_send, z_recv, y_send, y_recv, c_send, c_recv,
               rc_send, rc_recv, ry_send, ry_recv, rz_send, rz_recv):
    members = 2 * chips
    width = pa.shape[-1]
    piece = width // PIECES
    main_rows, tail_rows = members * MAIN, members * TAIL
    group = lax.axis_index("groups")
    me = lax.axis_index("dp")
    mine = lax.div(me, members)
    member = lax.rem(me, members)
    chip, core = lax.div(member, 2), lax.rem(member, 2)
    other = 1 - core

    def device(expert, chip_at, core_at):
        return (group, expert * members + chip_at * 2 + core_at)

    def expert_at(step):
        return lax.rem(mine + step, experts)

    def expert_before(step):
        return lax.rem(mine - step + experts, experts)

    def rows(core_at, chip_at, size, count):
        return pl.ds(pl.multiple_of((core_at * chips + chip_at) * size, size), count * size)

    loads = []
    for i, (src, dst) in enumerate(((wg_hbm, wg), (wu_hbm, wu), (wd_hbm, wd))):
        load = pltpu.make_async_copy(src, dst, load_sem.at[i])
        load.start()
        loads.append(load)
    own = [
        pltpu.make_async_copy(pa.at[mine], xf.at[mine, rows(core, chip, MAIN, 1)], own_sem.at[0]),
        pltpu.make_async_copy(pb.at[mine], xb.at[mine, rows(core, chip, 16, 1)], own_sem.at[1]),
    ]
    for copy in own:
        copy.start()

    partner = device(mine, chip, other)
    barrier = pltpu.get_barrier_semaphore()
    peers = [device(expert_at(s), chip, core) for s in range(1, experts)]
    peers += [device(mine, lax.rem(chip + d, chips), core) for d in range(1, chips)]
    peers += [partner]
    for peer in peers:
        pl.semaphore_signal(barrier, inc=1, device_id=peer, device_id_type=MESH)
    pl.semaphore_wait(barrier, len(peers))

    def send(pairs, sends, recvs, index, target):
        made = []
        for i, (src, dst) in enumerate(pairs):
            copy = pltpu.make_async_remote_copy(
                src_ref=src, dst_ref=dst, send_sem=sends.at[index, i], recv_sem=recvs.at[index, i],
                device_id=target, device_id_type=MESH)
            copy.start()
            made.append(copy)
        return made

    def arrive(copies):
        for copy in copies:
            copy.wait_recv()

    def sent(copies):
        for copy in copies:
            copy.wait_send()

    pending = []
    z_copies = {}
    for s in range(1, experts):
        to = expert_before(s)
        z_copies[s] = send(
            ((pa.at[to], xf.at[mine, rows(core, chip, MAIN, 1)]),
             (pb.at[to], xb.at[mine, rows(core, chip, 16, 1)])),
            z_send, z_recv, s, device(to, chip, core))
        pending += z_copies[s]

    y_copies, c_copies = {}, {}

    def spread(s):
        at = expert_at(s)
        if s == 0:
            for copy in own:
                copy.wait()
        else:
            arrive(z_copies[s])
        y_copies[s] = []
        for d in range(1, chips):
            a_ref = xf.at[at, rows(core, chip, MAIN, 1)]
            b_ref = xb.at[at, rows(core, chip, 16, 1)]
            y_copies[s] += send(((a_ref, a_ref), (b_ref, b_ref)), y_send, y_recv, s * chips + d,
                                device(mine, lax.rem(chip + d, chips), core))

    def forward(s):
        at = expert_at(s)
        arrive(y_copies[s])
        a_ref = xf.at[at, rows(core, 0, MAIN, chips)]
        b_ref = xb.at[at, rows(core, 0, 16, chips)]
        c_copies[s] = send(((a_ref, a_ref), (b_ref, b_ref)), c_send, c_recv, s, partner)

    out_rows = lax.broadcasted_iota(jnp.int32, (tail_rows, members * 16), 0)
    in_rows = lax.broadcasted_iota(jnp.int32, (tail_rows, members * 16), 1)
    back_out = lax.broadcasted_iota(jnp.int32, (members * 16, tail_rows), 0)
    back_in = lax.broadcasted_iota(jnp.int32, (members * 16, tail_rows), 1)

    def compute(s):
        at = expert_at(s)
        arrive(c_copies[s])
        sent(y_copies[s])
        sent(c_copies[s])
        for q in range(PIECES):
            pick = (in_rows == (out_rows // TAIL) * 16 + q * TAIL + out_rows % TAIL)
            moved = jnp.dot(pick.astype(jnp.bfloat16), xb[at], preferred_element_type=jnp.float32)
            xf[at, main_rows:main_rows + tail_rows, q * piece:(q + 1) * piece] = moved.astype(jnp.bfloat16)
        if s == 0:
            loads[0].wait()
            loads[1].wait()

        @pl.loop(0, hid.shape[1] // TILE)
        def _(j):
            cols = pl.ds(pl.multiple_of(j * TILE, TILE), TILE)
            gate = jnp.dot(xf[at], wg[:, cols], preferred_element_type=jnp.float32)
            up = jnp.dot(xf[at], wu[:, cols], preferred_element_type=jnp.float32)
            hid[:, cols] = (gate / (1.0 + jnp.exp(-gate)) * up).astype(jnp.bfloat16)

        if s == 0:
            loads[2].wait()

        @pl.loop(0, width // TILE)
        def _(j):
            cols = pl.ds(pl.multiple_of(j * TILE, TILE), TILE)
            xf[at, :, cols] = jnp.dot(hid[...], wd[:, cols], preferred_element_type=jnp.float32).astype(jnp.bfloat16)

        total = jnp.zeros((members * 16, piece), jnp.float32)
        for q in range(PIECES):
            place = (back_out == (back_in // TAIL) * 16 + q * TAIL + back_in % TAIL)
            total = total + jnp.dot(
                place.astype(jnp.bfloat16),
                xf[at, main_rows:main_rows + tail_rows, q * piece:(q + 1) * piece],
                preferred_element_type=jnp.float32)
        xb[at] = total.astype(jnp.bfloat16)

    rc_copies, ry_copies, rz_copies = {}, {}, {}

    def pair(s):
        at = expert_at(s)
        rc_copies[s] = send(
            ((xf.at[at, rows(other, 0, MAIN, chips)], cra.at[s]),
             (xb.at[at, rows(other, 0, 16, chips)], crb.at[s])),
            rc_send, rc_recv, s, partner)
        pending.extend(rc_copies[s])

    def across(s):
        at = expert_at(s)
        arrive(rc_copies[s])
        cra[s] = (cra[s].astype(jnp.float32)
                  + xf[at, rows(core, 0, MAIN, chips)].astype(jnp.float32)).astype(jnp.bfloat16)
        crb[s] = (crb[s].astype(jnp.float32)
                  + xb[at, rows(core, 0, 16, chips)].astype(jnp.float32)).astype(jnp.bfloat16)
        ry_copies[s] = []
        for d in range(1, chips):
            to = lax.rem(chip + d, chips)
            ry_copies[s] += send(
                ((cra.at[s, rows(0, to, MAIN, 1)], yra.at[s, d - 1]),
                 (crb.at[s, rows(0, to, 16, 1)], yrb.at[s, d - 1])),
                ry_send, ry_recv, s * chips + d, device(mine, to, core))
        pending.extend(ry_copies[s])

    def home(s):
        arrive(ry_copies[s])
        a_sum = cra[s, rows(0, chip, MAIN, 1)].astype(jnp.float32)
        b_sum = crb[s, rows(0, chip, 16, 1)].astype(jnp.float32)
        for d in range(1, chips):
            a_sum = a_sum + yra[s, d - 1].astype(jnp.float32)
            b_sum = b_sum + yrb[s, d - 1].astype(jnp.float32)
        if s == 0:
            ra[mine] = a_sum.astype(jnp.bfloat16)
            rb[mine] = b_sum.astype(jnp.bfloat16)
            return
        zsa[s] = a_sum.astype(jnp.bfloat16)
        zsb[s] = b_sum.astype(jnp.bfloat16)
        rz_copies[s] = send(((zsa.at[s], ra.at[mine]), (zsb.at[s], rb.at[mine])),
                            rz_send, rz_recv, s, device(expert_at(s), chip, core))
        pending.extend(rz_copies[s])

    spread(0)
    for s in range(experts):
        if s + 1 < experts:
            spread(s + 1)
        if s == 0:
            forward(0)
        compute(s)
        pair(s)
        if s + 1 < experts:
            forward(s + 1)
        if s >= 1:
            home(s - 1)
        across(s)
    home(experts - 1)
    for s in range(1, experts):
        arrive(rz_copies[s])
    sent(pending)


def exchange(packed_a, packed_b, w_gate, w_up, w_down, devices_dp):
    experts, _, width = packed_a.shape
    members = devices_dp // experts
    chips = members // 2
    piece = width // PIECES
    hidden = w_gate.shape[1]
    bf16 = jnp.bfloat16
    dma = pltpu.SemaphoreType.DMA
    vmem = pl.BlockSpec(memory_space=pltpu.VMEM)
    hbm = pl.BlockSpec(memory_space=pl.ANY)
    flops = experts * members * CAP * width * hidden * 6
    return pl.pallas_call(
        functools.partial(moe_kernel, experts, chips),
        out_shape=[jax.ShapeDtypeStruct((experts, MAIN, width), bf16),
                   jax.ShapeDtypeStruct((experts, 16, piece), bf16)],
        in_specs=[vmem, vmem, hbm, hbm, hbm],
        out_specs=[vmem, vmem],
        scratch_shapes=[
            pltpu.VMEM(w_gate.shape, bf16),
            pltpu.VMEM(w_up.shape, bf16),
            pltpu.VMEM(w_down.shape, bf16),
            pltpu.VMEM((experts, members * CAP, width), bf16),
            pltpu.VMEM((experts, members * 16, piece), bf16),
            pltpu.VMEM((members * CAP, hidden), bf16),
            pltpu.VMEM((experts, chips * MAIN, width), bf16),
            pltpu.VMEM((experts, chips * 16, piece), bf16),
            pltpu.VMEM((experts, chips - 1, MAIN, width), bf16),
            pltpu.VMEM((experts, chips - 1, 16, piece), bf16),
            pltpu.VMEM((experts, MAIN, width), bf16),
            pltpu.VMEM((experts, 16, piece), bf16),
            dma((3,)),
            dma((2,)),
            dma((experts, 2)), dma((experts, 2)),
            dma((experts * chips, 2)), dma((experts * chips, 2)),
            dma((experts, 2)), dma((experts, 2)),
            dma((experts, 2)), dma((experts, 2)),
            dma((experts * chips, 2)), dma((experts * chips, 2)),
            dma((experts, 2)), dma((experts, 2)),
        ],
        compiler_params=pltpu.CompilerParams(
            collective_id=0, has_side_effects=True, vmem_limit_bytes=60 * 1024 * 1024),
        cost_estimate=pl.CostEstimate(
            flops=flops, bytes_accessed=6 * width * hidden, transcendentals=0),
    )(packed_a, packed_b, w_gate, w_up, w_down)


def local(tokens, router, routes, w_gate, w_up, w_down):
    tok_rows, width = tokens.shape
    experts = router.shape[1]
    top_count = routes.shape[1]
    devices_dp = lax.axis_size("dp")
    logits = jnp.dot(tokens, router, preferred_element_type=jnp.float32)
    onehot = routes[:, :, None] == jnp.arange(experts, dtype=jnp.int32)[None, None, :]
    picked = jnp.sum(jnp.where(onehot, logits[:, None, :], 0.0), axis=2)
    first_share = jax.nn.sigmoid(picked[:, 0] - picked[:, 1])
    shares = jnp.stack([first_share, 1.0 - first_share], axis=1)
    flat_hot = onehot.reshape(tok_rows * top_count, experts).astype(jnp.int32)
    before = jnp.cumsum(flat_hot, axis=0) - flat_hot
    slot_index = jnp.sum(before * flat_hot, axis=1)
    target = routes.reshape(-1) * CAP + slot_index
    select = target[None, :] == jnp.arange(experts * CAP, dtype=jnp.int32)[:, None]
    by_token = select.reshape(experts * CAP, tok_rows, top_count)
    token_select = jnp.any(by_token, axis=2)
    packed = jnp.dot(token_select.astype(jnp.bfloat16), tokens, preferred_element_type=jnp.float32)
    packed = packed.astype(jnp.bfloat16).reshape(experts, CAP, width)
    piece = width // PIECES
    tail = packed[:, MAIN:].reshape(experts, TAIL, PIECES, piece).transpose(0, 2, 1, 3)
    back_a, back_b = exchange(packed[:, :MAIN], tail.reshape(experts, 16, piece), w_gate, w_up, w_down, devices_dp)
    back_tail = back_b.reshape(experts, PIECES, TAIL, piece).transpose(0, 2, 1, 3).reshape(experts, TAIL, width)
    flat_back = jnp.concatenate([back_a, back_tail], axis=1).reshape(experts * CAP, width)
    weights = jnp.sum(jnp.where(by_token, shares[None], 0.0), axis=2)
    mixed = jnp.dot(weights.T, flat_back.astype(jnp.float32), precision=lax.Precision.HIGHEST)
    return mixed.astype(jnp.bfloat16)


def solution(mesh):
    placed = (
        P(("groups", "dp"), None),
        P(),
        P(("groups", "dp"), None),
        P(None, "dp"),
        P(None, "dp"),
        P("dp", None),
    )
    return jax.shard_map(
        local, mesh=mesh, in_specs=placed, out_specs=P(("groups", "dp"), None), check_vma=False
    )
```

```python
import functools

import jax
import jax.numpy as jnp
from jax import lax
from jax.experimental import pallas as pl
from jax.experimental.pallas import tpu as pltpu
from jax.sharding import PartitionSpec as P

CAP = 36
MAIN = 32
TAIL = CAP - MAIN
PIECES = 16 // TAIL
MESH = pl.DeviceIdType.MESH
TILE = 512


def moe_kernel(experts, chips, tokens, routes, router, wg_hbm, wu_hbm, wd_hbm, mixed,
               pa, pb, ra, rb, wg, wu, wd, xf, xb, hid, cra, crb, yra, yrb, zsa, zsb,
               load_sem, own_sem, z_send, z_recv, y_send, y_recv, c_send, c_recv,
               rc_send, rc_recv, ry_send, ry_recv, rz_send, rz_recv):
    members = 2 * chips
    width = pa.shape[-1]
    piece = width // PIECES
    main_rows, tail_rows = members * MAIN, members * TAIL
    group = lax.axis_index("groups")
    me = lax.axis_index("dp")
    mine = lax.div(me, members)
    member = lax.rem(me, members)
    chip, core = lax.div(member, 2), lax.rem(member, 2)
    other = 1 - core

    def device(expert, chip_at, core_at):
        return (group, expert * members + chip_at * 2 + core_at)

    def expert_at(step):
        return lax.rem(mine + step, experts)

    def expert_before(step):
        return lax.rem(mine - step + experts, experts)

    def rows(core_at, chip_at, size, count):
        return pl.ds(pl.multiple_of((core_at * chips + chip_at) * size, size), count * size)

    hidden = hid.shape[1]
    step_cols = min(TILE, hidden)
    steps = hidden // step_cols

    def cols_at(j, size):
        return pl.ds(pl.multiple_of(j * size, size), size)

    def load_in(j):
        cols = cols_at(j, step_cols)
        return [pltpu.make_async_copy(wg_hbm.at[:, cols], wg.at[:, cols], load_sem.at[2 * j]),
                pltpu.make_async_copy(wu_hbm.at[:, cols], wu.at[:, cols], load_sem.at[2 * j + 1])]

    load_down = pltpu.make_async_copy(wd_hbm, wd, load_sem.at[2 * steps])
    for j in range(steps):
        for load in load_in(j):
            load.start()
    load_down.start()

    partner = device(mine, chip, other)
    barrier = pltpu.get_barrier_semaphore()
    peers = [device(expert_at(s), chip, core) for s in range(1, experts)]
    peers += [device(mine, lax.rem(chip + d, chips), core) for d in range(1, chips)]
    peers += [partner]
    for peer in peers:
        pl.semaphore_signal(barrier, inc=1, device_id=peer, device_id_type=MESH)

    tok_rows = tokens.shape[0]
    f32, bf16 = jnp.float32, jnp.bfloat16
    first, second = routes[0:1, :], routes[1:2, :]
    expert_row = lax.broadcasted_iota(jnp.int32, (experts, tok_rows), 0)
    named = (expert_row == first) | (expert_row == second)
    earlier = (lax.broadcasted_iota(jnp.int32, (tok_rows, tok_rows), 0)
               < lax.broadcasted_iota(jnp.int32, (tok_rows, tok_rows), 1))
    slot = jnp.dot(jnp.where(named, 1.0, 0.0).astype(bf16), jnp.where(earlier, 1.0, 0.0).astype(bf16),
                   preferred_element_type=f32)
    slot = jnp.where(named, slot, -1.0).astype(jnp.int32)
    main_slot = lax.broadcasted_iota(jnp.int32, (MAIN, tok_rows), 0)
    tail_slot = lax.broadcasted_iota(jnp.int32, (16, tok_rows), 0)

    def main_values(values):
        return jnp.concatenate(
            [jnp.where(slot[e:e + 1, :] == main_slot, values[e:e + 1, :], 0.0) for e in range(experts)], axis=0)

    def tail_values(values, q):
        wanted = jnp.where(tail_slot // TAIL == q, MAIN + tail_slot % TAIL, -2)
        return jnp.concatenate(
            [jnp.where(slot[e:e + 1, :] == wanted, values[e:e + 1, :], 0.0) for e in range(experts)], axis=0)

    ones = jnp.ones((experts, tok_rows), f32)
    pick_main = main_values(ones).astype(bf16)
    pick_tail = [tail_values(ones, q).astype(bf16) for q in range(PIECES)]
    for j in range(PIECES):
        cols = slice(j * piece, (j + 1) * piece)
        block = jnp.dot(pick_main, tokens[:, cols], preferred_element_type=f32).astype(bf16)
        pa[:, :, cols] = block.reshape(experts, MAIN, piece)
    tails = jnp.zeros((experts * 16, piece), f32)
    for q in range(PIECES):
        tails = tails + jnp.dot(pick_tail[q], tokens[:, q * piece:(q + 1) * piece], preferred_element_type=f32)
    pb[...] = tails.astype(bf16).reshape(experts, 16, piece)

    own = [
        pltpu.make_async_copy(pa.at[mine], xf.at[mine, rows(core, chip, MAIN, 1)], own_sem.at[0]),
        pltpu.make_async_copy(pb.at[mine], xb.at[mine, rows(core, chip, 16, 1)], own_sem.at[1]),
    ]
    for copy in own:
        copy.start()
    pl.semaphore_wait(barrier, len(peers))

    def send(pairs, sends, recvs, index, target):
        made = []
        for i, (src, dst) in enumerate(pairs):
            copy = pltpu.make_async_remote_copy(
                src_ref=src, dst_ref=dst, send_sem=sends.at[index, i], recv_sem=recvs.at[index, i],
                device_id=target, device_id_type=MESH)
            copy.start()
            made.append(copy)
        return made

    def arrive(copies):
        for copy in copies:
            copy.wait_recv()

    def sent(copies):
        for copy in copies:
            copy.wait_send()

    pending = []
    z_copies = {}

    def dispatch(s):
        to = expert_before(s)
        if s > 1:
            sent(z_copies[s - 1][:1])
        z_copies[s] = send(
            ((pa.at[to], xf.at[mine, rows(core, chip, MAIN, 1)]),
             (pb.at[to], xb.at[mine, rows(core, chip, 16, 1)])),
            z_send, z_recv, s, device(to, chip, core))
        pending.extend(z_copies[s] if s == experts - 1 else z_copies[s][1:])

    y_copies, c_copies = {}, {}

    def spread(s):
        at = expert_at(s)
        if s == 0:
            for copy in own:
                copy.wait()
        else:
            arrive(z_copies[s])
        y_copies[s] = []
        for d in range(1, chips):
            a_ref = xf.at[at, rows(core, chip, MAIN, 1)]
            b_ref = xb.at[at, rows(core, chip, 16, 1)]
            y_copies[s] += send(((a_ref, a_ref), (b_ref, b_ref)), y_send, y_recv, s * chips + d,
                                device(mine, lax.rem(chip + d, chips), core))

    def forward(s):
        at = expert_at(s)
        arrive(y_copies[s])
        a_ref = xf.at[at, rows(core, 0, MAIN, chips)]
        b_ref = xb.at[at, rows(core, 0, 16, chips)]
        c_copies[s] = send(((a_ref, a_ref), (b_ref, b_ref)), c_send, c_recv, s, partner)

    out_rows = lax.broadcasted_iota(jnp.int32, (tail_rows, members * 16), 0)
    in_rows = lax.broadcasted_iota(jnp.int32, (tail_rows, members * 16), 1)
    back_out = lax.broadcasted_iota(jnp.int32, (members * 16, tail_rows), 0)
    back_in = lax.broadcasted_iota(jnp.int32, (members * 16, tail_rows), 1)

    def hidden_units(s, begin, end):
        at = expert_at(s)
        if begin == 0:
            arrive(c_copies[s])
            for q in range(PIECES):
                pick = (in_rows == (out_rows // TAIL) * 16 + q * TAIL + out_rows % TAIL)
                moved = jnp.dot(pick.astype(bf16), xb[at], preferred_element_type=f32)
                xf[at, main_rows:main_rows + tail_rows, q * piece:(q + 1) * piece] = moved.astype(bf16)
        if begin == end:
            return

        @pl.loop(begin, end)
        def _(j):
            if s == 0:
                for load in load_in(j):
                    load.wait()
            cols = cols_at(j, step_cols)
            gate = jnp.dot(xf[at], wg[:, cols], preferred_element_type=f32)
            up = jnp.dot(xf[at], wu[:, cols], preferred_element_type=f32)
            hid[:, cols] = (gate / (1.0 + jnp.exp(-gate)) * up).astype(bf16)

    def down(s):
        at = expert_at(s)
        sent(y_copies[s])
        sent(c_copies[s])
        if s == 0:
            load_down.wait()

        @pl.loop(0, width // TILE)
        def _(j):
            cols = cols_at(j, TILE)
            xf[at, :, cols] = jnp.dot(hid[...], wd[:, cols], preferred_element_type=f32).astype(bf16)

        total = jnp.zeros((members * 16, piece), jnp.float32)
        for q in range(PIECES):
            place = (back_out == (back_in // TAIL) * 16 + q * TAIL + back_in % TAIL)
            total = total + jnp.dot(
                place.astype(jnp.bfloat16),
                xf[at, main_rows:main_rows + tail_rows, q * piece:(q + 1) * piece],
                preferred_element_type=jnp.float32)
        xb[at] = total.astype(jnp.bfloat16)

    rc_copies, ry_copies, rz_copies = {}, {}, {}

    def pair(s):
        at = expert_at(s)
        rc_copies[s] = send(
            ((xf.at[at, rows(other, 0, MAIN, chips)], cra.at[s]),
             (xb.at[at, rows(other, 0, 16, chips)], crb.at[s])),
            rc_send, rc_recv, s, partner)
        pending.extend(rc_copies[s])

    def across(s):
        at = expert_at(s)
        arrive(rc_copies[s])
        cra[s] = (cra[s].astype(jnp.float32)
                  + xf[at, rows(core, 0, MAIN, chips)].astype(jnp.float32)).astype(jnp.bfloat16)
        crb[s] = (crb[s].astype(jnp.float32)
                  + xb[at, rows(core, 0, 16, chips)].astype(jnp.float32)).astype(jnp.bfloat16)
        ry_copies[s] = []
        for d in range(1, chips):
            to = lax.rem(chip + d, chips)
            ry_copies[s] += send(
                ((cra.at[s, rows(0, to, MAIN, 1)], yra.at[s, d - 1]),
                 (crb.at[s, rows(0, to, 16, 1)], yrb.at[s, d - 1])),
                ry_send, ry_recv, s * chips + d, device(mine, to, core))
        pending.extend(ry_copies[s])

    def home(s):
        arrive(ry_copies[s])
        a_sum = cra[s, rows(0, chip, MAIN, 1)].astype(jnp.float32)
        b_sum = crb[s, rows(0, chip, 16, 1)].astype(jnp.float32)
        for d in range(1, chips):
            a_sum = a_sum + yra[s, d - 1].astype(jnp.float32)
            b_sum = b_sum + yrb[s, d - 1].astype(jnp.float32)
        if s == 0:
            ra[mine] = a_sum.astype(jnp.bfloat16)
            rb[mine] = b_sum.astype(jnp.bfloat16)
            return
        zsa[s] = a_sum.astype(jnp.bfloat16)
        zsb[s] = b_sum.astype(jnp.bfloat16)
        rz_copies[s] = send(((zsa.at[s], ra.at[mine]), (zsb.at[s], rb.at[mine])),
                            rz_send, rz_recv, s, device(expert_at(s), chip, core))
        pending.extend(rz_copies[s])

    dispatch(1)
    spread(0)
    forward(0)
    if experts > 2:
        dispatch(2)
    spread(1)
    for s in range(experts):
        hidden_units(s, 0, 1)
        if s >= 1:
            across(s - 1)
        if s >= 2:
            home(s - 2)
        if steps > 1:
            hidden_units(s, 1, steps)
        if s + 1 < experts:
            forward(s + 1)
        down(s)
        pair(s)
        if s + 3 < experts:
            dispatch(s + 3)
        if s + 2 < experts:
            spread(s + 2)
    home(experts - 2)
    across(experts - 1)

    logits = lax.dot_general(router[...], tokens[...], (((1,), (1,)), ((), ())), preferred_element_type=f32)
    gap = jnp.sum(jnp.where(expert_row == first, logits, 0.0) - jnp.where(expert_row == second, logits, 0.0),
                  axis=0, keepdims=True)
    share = 1.0 / (1.0 + jnp.exp(-gap))
    shares = jnp.where(expert_row == first, share, 1.0 - share)

    def parts(values):
        high = values.astype(bf16)
        left = values - high.astype(f32)
        middle = left.astype(bf16)
        return high, middle, (left - middle.astype(f32)).astype(bf16)

    def weighted(pieces, data):
        return sum(lax.dot_general(p, data, (((0,), (0,)), ((), ())), preferred_element_type=f32) for p in pieces)

    main_shares = parts(main_values(shares))
    tail_shares = [parts(tail_values(shares, q)) for q in range(PIECES)]
    home(experts - 1)
    for s in range(1, experts):
        arrive(rz_copies[s])
    tail_data = rb[...].reshape(experts * 16, piece)
    for q in range(PIECES):
        cols = slice(q * piece, (q + 1) * piece)
        main_data = ra[:, :, cols].reshape(experts * MAIN, piece)
        mixed[:, cols] = (weighted(main_shares, main_data) + weighted(tail_shares[q], tail_data)).astype(bf16)
    sent(pending)


def local(tokens, router, routes, w_gate, w_up, w_down):
    tok_rows, width = tokens.shape
    experts = router.shape[1]
    devices_dp = lax.axis_size("dp")
    members = devices_dp // experts
    chips = members // 2
    piece = width // PIECES
    hidden = w_gate.shape[1]
    bf16 = jnp.bfloat16
    dma = pltpu.SemaphoreType.DMA
    vmem = pl.BlockSpec(memory_space=pltpu.VMEM)
    hbm = pl.BlockSpec(memory_space=pl.ANY)
    flops = experts * members * CAP * width * hidden * 6
    return pl.pallas_call(
        functools.partial(moe_kernel, experts, chips),
        out_shape=jax.ShapeDtypeStruct((tok_rows, width), bf16),
        in_specs=[vmem, vmem, vmem, hbm, hbm, hbm],
        out_specs=vmem,
        scratch_shapes=[
            pltpu.VMEM((experts, MAIN, width), bf16),
            pltpu.VMEM((experts, 16, piece), bf16),
            pltpu.VMEM((experts, MAIN, width), bf16),
            pltpu.VMEM((experts, 16, piece), bf16),
            pltpu.VMEM(w_gate.shape, bf16),
            pltpu.VMEM(w_up.shape, bf16),
            pltpu.VMEM(w_down.shape, bf16),
            pltpu.VMEM((experts, members * CAP, width), bf16),
            pltpu.VMEM((experts, members * 16, piece), bf16),
            pltpu.VMEM((members * CAP, hidden), bf16),
            pltpu.VMEM((experts, chips * MAIN, width), bf16),
            pltpu.VMEM((experts, chips * 16, piece), bf16),
            pltpu.VMEM((experts, chips - 1, MAIN, width), bf16),
            pltpu.VMEM((experts, chips - 1, 16, piece), bf16),
            pltpu.VMEM((experts, MAIN, width), bf16),
            pltpu.VMEM((experts, 16, piece), bf16),
            dma((2 * (hidden // min(TILE, hidden)) + 1,)),
            dma((2,)),
            dma((experts, 2)), dma((experts, 2)),
            dma((experts * chips, 2)), dma((experts * chips, 2)),
            dma((experts, 2)), dma((experts, 2)),
            dma((experts, 2)), dma((experts, 2)),
            dma((experts * chips, 2)), dma((experts * chips, 2)),
            dma((experts, 2)), dma((experts, 2)),
        ],
        compiler_params=pltpu.CompilerParams(
            collective_id=0, has_side_effects=True, vmem_limit_bytes=60 * 1024 * 1024),
        cost_estimate=pl.CostEstimate(
            flops=flops, bytes_accessed=6 * width * hidden, transcendentals=0),
    )(tokens, routes.T, router.T, w_gate, w_up, w_down)


def solution(mesh):
    placed = (
        P(("groups", "dp"), None),
        P(),
        P(("groups", "dp"), None),
        P(None, "dp"),
        P(None, "dp"),
        P("dp", None),
    )
    return jax.shard_map(
        local, mesh=mesh, in_specs=placed, out_specs=P(("groups", "dp"), None), check_vma=False
    )
```

```python
import functools

import jax
import jax.numpy as jnp
from jax import lax
from jax.experimental import pallas as pl
from jax.experimental.pallas import tpu as pltpu
from jax.sharding import PartitionSpec as P

CAP = 36
MAIN = 32
TAIL = CAP - MAIN
PIECES = 16 // TAIL
MESH = pl.DeviceIdType.MESH
TILE = 512


def moe_kernel(experts, chips, tokens, routes, router, wg_hbm, wu_hbm, wd_hbm, mixed,
               pa, pb, ra, rb, wg, wu, wd, xf, xb, hid, cra, crb, yra, yrb, zsa, zsb,
               load_sem, own_sem, z_send, z_recv, y_send, y_recv, c_send, c_recv,
               rc_send, rc_recv, ry_send, ry_recv, rz_send, rz_recv):
    members = 2 * chips
    width = pa.shape[-1]
    piece = width // PIECES
    main_rows, tail_rows = members * MAIN, members * TAIL
    group = lax.axis_index("groups")
    me = lax.axis_index("dp")
    mine = lax.div(me, members)
    member = lax.rem(me, members)
    chip, core = lax.div(member, 2), lax.rem(member, 2)
    other = 1 - core

    def device(expert, chip_at, core_at):
        return (group, expert * members + chip_at * 2 + core_at)

    def expert_at(step):
        return lax.rem(mine + step, experts)

    def expert_before(step):
        return lax.rem(mine - step + experts, experts)

    def rows(core_at, chip_at, size, count):
        return pl.ds(pl.multiple_of((core_at * chips + chip_at) * size, size), count * size)

    hidden = hid.shape[1]
    step_cols = min(TILE, hidden)
    steps = hidden // step_cols

    def cols_at(j, size):
        return pl.ds(pl.multiple_of(j * size, size), size)

    def load_in(j):
        cols = cols_at(j, step_cols)
        return [pltpu.make_async_copy(wg_hbm.at[:, cols], wg.at[:, cols], load_sem.at[2 * j]),
                pltpu.make_async_copy(wu_hbm.at[:, cols], wu.at[:, cols], load_sem.at[2 * j + 1])]

    load_down = pltpu.make_async_copy(wd_hbm, wd, load_sem.at[2 * steps])
    for j in range(steps):
        for load in load_in(j):
            load.start()
    load_down.start()

    partner = device(mine, chip, other)
    barrier = pltpu.get_barrier_semaphore()
    peers = [device(expert_at(s), chip, core) for s in range(1, experts)]
    peers += [device(mine, lax.rem(chip + d, chips), core) for d in range(1, chips)]
    peers += [partner]
    for peer in peers:
        pl.semaphore_signal(barrier, inc=1, device_id=peer, device_id_type=MESH)

    tok_rows = tokens.shape[0]
    f32, bf16 = jnp.float32, jnp.bfloat16
    first, second = routes[0:1, :], routes[1:2, :]
    expert_row = lax.broadcasted_iota(jnp.int32, (experts, tok_rows), 0)
    named = (expert_row == first) | (expert_row == second)
    earlier = (lax.broadcasted_iota(jnp.int32, (tok_rows, tok_rows), 0)
               < lax.broadcasted_iota(jnp.int32, (tok_rows, tok_rows), 1))
    slot = jnp.dot(jnp.where(named, 1.0, 0.0).astype(bf16), jnp.where(earlier, 1.0, 0.0).astype(bf16),
                   preferred_element_type=f32)
    slot = jnp.where(named, slot, -1.0).astype(jnp.int32)
    main_slot = lax.broadcasted_iota(jnp.int32, (MAIN, tok_rows), 0)
    tail_slot = lax.broadcasted_iota(jnp.int32, (16, tok_rows), 0)

    def main_values(values):
        return jnp.concatenate(
            [jnp.where(slot[e:e + 1, :] == main_slot, values[e:e + 1, :], 0.0) for e in range(experts)], axis=0)

    def tail_values(values, q):
        wanted = jnp.where(tail_slot // TAIL == q, MAIN + tail_slot % TAIL, -2)
        return jnp.concatenate(
            [jnp.where(slot[e:e + 1, :] == wanted, values[e:e + 1, :], 0.0) for e in range(experts)], axis=0)

    ones = jnp.ones((experts, tok_rows), f32)
    pick_main = main_values(ones).astype(bf16)
    pick_tail = [tail_values(ones, q).astype(bf16) for q in range(PIECES)]
    for j in range(PIECES):
        cols = slice(j * piece, (j + 1) * piece)
        block = jnp.dot(pick_main, tokens[:, cols], preferred_element_type=f32).astype(bf16)
        pa[:, :, cols] = block.reshape(experts, MAIN, piece)
    tails = jnp.zeros((experts * 16, piece), f32)
    for q in range(PIECES):
        tails = tails + jnp.dot(pick_tail[q], tokens[:, q * piece:(q + 1) * piece], preferred_element_type=f32)
    pb[...] = tails.astype(bf16).reshape(experts, 16, piece)

    own = [
        pltpu.make_async_copy(pa.at[mine], xf.at[mine, rows(core, chip, MAIN, 1)], own_sem.at[0]),
        pltpu.make_async_copy(pb.at[mine], xb.at[mine, rows(core, chip, 16, 1)], own_sem.at[1]),
    ]
    for copy in own:
        copy.start()
    pl.semaphore_wait(barrier, len(peers))

    def send(pairs, sends, recvs, index, target):
        made = []
        for i, (src, dst) in enumerate(pairs):
            copy = pltpu.make_async_remote_copy(
                src_ref=src, dst_ref=dst, send_sem=sends.at[index, i], recv_sem=recvs.at[index, i],
                device_id=target, device_id_type=MESH)
            copy.start()
            made.append(copy)
        return made

    def arrive(copies):
        for copy in copies:
            copy.wait_recv()

    def sent(copies):
        for copy in copies:
            copy.wait_send()

    pending = []
    z_copies = {}

    def dispatch(s):
        to = expert_before(s)
        if s > 1:
            sent(z_copies[s - 1][:1])
        z_copies[s] = send(
            ((pa.at[to], xf.at[mine, rows(core, chip, MAIN, 1)]),
             (pb.at[to], xb.at[mine, rows(core, chip, 16, 1)])),
            z_send, z_recv, s, device(to, chip, core))
        pending.extend(z_copies[s] if s == experts - 1 else z_copies[s][1:])

    y_copies, c_copies = {}, {}

    def spread(s):
        at = expert_at(s)
        if s == 0:
            for copy in own:
                copy.wait()
        else:
            arrive(z_copies[s])
        y_copies[s] = []
        for d in range(1, chips):
            a_ref = xf.at[at, rows(core, chip, MAIN, 1)]
            b_ref = xb.at[at, rows(core, chip, 16, 1)]
            y_copies[s] += send(((a_ref, a_ref), (b_ref, b_ref)), y_send, y_recv, s * chips + d,
                                device(mine, lax.rem(chip + d, chips), core))

    def forward(s):
        at = expert_at(s)
        arrive(y_copies[s])
        a_ref = xf.at[at, rows(core, 0, MAIN, chips)]
        b_ref = xb.at[at, rows(core, 0, 16, chips)]
        c_copies[s] = send(((a_ref, a_ref), (b_ref, b_ref)), c_send, c_recv, s, partner)

    out_rows = lax.broadcasted_iota(jnp.int32, (tail_rows, members * 16), 0)
    in_rows = lax.broadcasted_iota(jnp.int32, (tail_rows, members * 16), 1)
    back_out = lax.broadcasted_iota(jnp.int32, (members * 16, tail_rows), 0)
    back_in = lax.broadcasted_iota(jnp.int32, (members * 16, tail_rows), 1)

    def hidden_units(s, begin, end):
        at = expert_at(s)
        if begin == 0:
            arrive(c_copies[s])
            for q in range(PIECES):
                pick = (in_rows == (out_rows // TAIL) * 16 + q * TAIL + out_rows % TAIL)
                moved = jnp.dot(pick.astype(bf16), xb[at], preferred_element_type=f32)
                xf[at, main_rows:main_rows + tail_rows, q * piece:(q + 1) * piece] = moved.astype(bf16)
        if begin == end:
            return

        @pl.loop(begin, end)
        def _(j):
            if s == 0:
                for load in load_in(j):
                    load.wait()
            cols = cols_at(j, step_cols)
            gate = jnp.dot(xf[at], wg[:, cols], preferred_element_type=f32)
            up = jnp.dot(xf[at], wu[:, cols], preferred_element_type=f32)
            hid[:, cols] = (gate / (1.0 + jnp.exp(-gate)) * up).astype(bf16)

    def down(s):
        at = expert_at(s)
        sent(y_copies[s])
        sent(c_copies[s])
        if s == 0:
            load_down.wait()

        @pl.loop(0, width // TILE)
        def _(j):
            cols = cols_at(j, TILE)
            xf[at, :, cols] = jnp.dot(hid[...], wd[:, cols], preferred_element_type=f32).astype(bf16)

        total = jnp.zeros((members * 16, piece), jnp.float32)
        for q in range(PIECES):
            place = (back_out == (back_in // TAIL) * 16 + q * TAIL + back_in % TAIL)
            total = total + jnp.dot(
                place.astype(jnp.bfloat16),
                xf[at, main_rows:main_rows + tail_rows, q * piece:(q + 1) * piece],
                preferred_element_type=jnp.float32)
        xb[at] = total.astype(jnp.bfloat16)

    rc_copies, ry_copies, rz_copies = {}, {}, {}

    def pair(s):
        at = expert_at(s)
        rc_copies[s] = send(
            ((xf.at[at, rows(other, 0, MAIN, chips)], cra.at[s]),
             (xb.at[at, rows(other, 0, 16, chips)], crb.at[s])),
            rc_send, rc_recv, s, partner)
        pending.extend(rc_copies[s])

    def across(s):
        at = expert_at(s)
        arrive(rc_copies[s])
        cra[s] = (cra[s].astype(jnp.float32)
                  + xf[at, rows(core, 0, MAIN, chips)].astype(jnp.float32)).astype(jnp.bfloat16)
        crb[s] = (crb[s].astype(jnp.float32)
                  + xb[at, rows(core, 0, 16, chips)].astype(jnp.float32)).astype(jnp.bfloat16)
        ry_copies[s] = []
        for d in range(1, chips):
            to = lax.rem(chip + d, chips)
            ry_copies[s] += send(
                ((cra.at[s, rows(0, to, MAIN, 1)], yra.at[s, d - 1]),
                 (crb.at[s, rows(0, to, 16, 1)], yrb.at[s, d - 1])),
                ry_send, ry_recv, s * chips + d, device(mine, to, core))
        pending.extend(ry_copies[s])

    def home(s):
        arrive(ry_copies[s])
        a_sum = cra[s, rows(0, chip, MAIN, 1)].astype(jnp.float32)
        b_sum = crb[s, rows(0, chip, 16, 1)].astype(jnp.float32)
        for d in range(1, chips):
            a_sum = a_sum + yra[s, d - 1].astype(jnp.float32)
            b_sum = b_sum + yrb[s, d - 1].astype(jnp.float32)
        if s == 0:
            ra[mine] = a_sum.astype(jnp.bfloat16)
            rb[mine] = b_sum.astype(jnp.bfloat16)
            return
        zsa[s] = a_sum.astype(jnp.bfloat16)
        zsb[s] = b_sum.astype(jnp.bfloat16)
        rz_copies[s] = send(((zsa.at[s], ra.at[mine]), (zsb.at[s], rb.at[mine])),
                            rz_send, rz_recv, s, device(expert_at(s), chip, core))
        pending.extend(rz_copies[s])

    dispatch(1)
    spread(0)
    forward(0)
    if experts > 2:
        dispatch(2)
    spread(1)
    for s in range(experts):
        hidden_units(s, 0, 1)
        if s >= 2:
            across(s - 1)
        if s >= 3:
            home(s - 2)
        if steps > 1:
            hidden_units(s, 1, steps)
        if s + 1 < experts:
            forward(s + 1)
        if s == max(1, experts - 2):
            across(0)
        down(s)
        pair(s)
        if s + 3 < experts:
            dispatch(s + 3)
        if s + 2 < experts:
            spread(s + 2)
    home(experts - 2)
    across(experts - 1)
    home(0)

    logits = lax.dot_general(router[...], tokens[...], (((1,), (1,)), ((), ())), preferred_element_type=f32)
    gap = jnp.sum(jnp.where(expert_row == first, logits, 0.0) - jnp.where(expert_row == second, logits, 0.0),
                  axis=0, keepdims=True)
    share = 1.0 / (1.0 + jnp.exp(-gap))
    shares = jnp.where(expert_row == first, share, 1.0 - share)

    def parts(values):
        high = values.astype(bf16)
        left = values - high.astype(f32)
        middle = left.astype(bf16)
        return high, middle, (left - middle.astype(f32)).astype(bf16)

    def weighted(pieces, data):
        return sum(lax.dot_general(p, data, (((0,), (0,)), ((), ())), preferred_element_type=f32) for p in pieces)

    main_shares = parts(main_values(shares))
    tail_shares = [parts(tail_values(shares, q)) for q in range(PIECES)]
    home(experts - 1)
    for s in range(1, experts):
        arrive(rz_copies[s])
    tail_data = rb[...].reshape(experts * 16, piece)
    for q in range(PIECES):
        cols = slice(q * piece, (q + 1) * piece)
        main_data = ra[:, :, cols].reshape(experts * MAIN, piece)
        mixed[:, cols] = (weighted(main_shares, main_data) + weighted(tail_shares[q], tail_data)).astype(bf16)
    sent(pending)


def local(tokens, router, routes, w_gate, w_up, w_down):
    tok_rows, width = tokens.shape
    experts = router.shape[1]
    devices_dp = lax.axis_size("dp")
    members = devices_dp // experts
    chips = members // 2
    piece = width // PIECES
    hidden = w_gate.shape[1]
    bf16 = jnp.bfloat16
    dma = pltpu.SemaphoreType.DMA
    vmem = pl.BlockSpec(memory_space=pltpu.VMEM)
    hbm = pl.BlockSpec(memory_space=pl.ANY)
    flops = experts * members * CAP * width * hidden * 6
    return pl.pallas_call(
        functools.partial(moe_kernel, experts, chips),
        out_shape=jax.ShapeDtypeStruct((tok_rows, width), bf16),
        in_specs=[vmem, vmem, vmem, hbm, hbm, hbm],
        out_specs=vmem,
        scratch_shapes=[
            pltpu.VMEM((experts, MAIN, width), bf16),
            pltpu.VMEM((experts, 16, piece), bf16),
            pltpu.VMEM((experts, MAIN, width), bf16),
            pltpu.VMEM((experts, 16, piece), bf16),
            pltpu.VMEM(w_gate.shape, bf16),
            pltpu.VMEM(w_up.shape, bf16),
            pltpu.VMEM(w_down.shape, bf16),
            pltpu.VMEM((experts, members * CAP, width), bf16),
            pltpu.VMEM((experts, members * 16, piece), bf16),
            pltpu.VMEM((members * CAP, hidden), bf16),
            pltpu.VMEM((experts, chips * MAIN, width), bf16),
            pltpu.VMEM((experts, chips * 16, piece), bf16),
            pltpu.VMEM((experts, chips - 1, MAIN, width), bf16),
            pltpu.VMEM((experts, chips - 1, 16, piece), bf16),
            pltpu.VMEM((experts, MAIN, width), bf16),
            pltpu.VMEM((experts, 16, piece), bf16),
            dma((2 * (hidden // min(TILE, hidden)) + 1,)),
            dma((2,)),
            dma((experts, 2)), dma((experts, 2)),
            dma((experts * chips, 2)), dma((experts * chips, 2)),
            dma((experts, 2)), dma((experts, 2)),
            dma((experts, 2)), dma((experts, 2)),
            dma((experts * chips, 2)), dma((experts * chips, 2)),
            dma((experts, 2)), dma((experts, 2)),
        ],
        compiler_params=pltpu.CompilerParams(
            collective_id=0, has_side_effects=True, vmem_limit_bytes=60 * 1024 * 1024),
        cost_estimate=pl.CostEstimate(
            flops=flops, bytes_accessed=6 * width * hidden, transcendentals=0),
    )(tokens, routes.T, router.T, w_gate, w_up, w_down)


def solution(mesh):
    placed = (
        P(("groups", "dp"), None),
        P(),
        P(("groups", "dp"), None),
        P(None, "dp"),
        P(None, "dp"),
        P("dp", None),
    )
    return jax.shard_map(
        local, mesh=mesh, in_specs=placed, out_specs=P(("groups", "dp"), None), check_vma=False
    )
```
